32 devices in a mesh: grp: 4 (over y, x), shard: 8 (over z, core).
Axes of the slice: x: 2, y: 2, z: 4, core: 2. Of those that a mesh axis runs over, the one named last changes fastest.
Arguments:
- points: bfloat16 [4, 12288, 1024], P('grp', 'shard'), may hold values from -6 to 6
- centroids: bfloat16 [4, 1024, 1024], P('grp', 'shard'), may hold values from -1.5 to 1.5
- tile_counts: int32 [4], replicated, may hold values from 49 to 96, as said below
Outputs:
- new_centroids: float32 [4, 1024, 1024], P('grp', 'shard')
- posterior_rows: bfloat16 [4, 12288, 1024], P('grp', 'shard')
The draws below stay inside these ranges and needn't reach their ends.
Inputs may be any that keep to these rules, and one draw needn't show every extreme that they name: `tile_counts`: every coarse cluster has more than half of its 96 tile slots live, and some cluster has all 96.
All inputs are finite; a program needn't handle non-finite values.
Results may differ from the reference program's by a relative error of at most 0.0076.
Values may be sent and summed in bfloat16 or wider, within the bound.
No kernel may reach another device: no remote copies, remote signals or barrier semaphores. Data moves between devices by JAX's collectives and lax.ppermute only.
A program may use at most 64 MiB of HBM per device.

```python
import jax
import jax.numpy as jnp
from jax import lax

EMBED_WIDTH = 1024
K = 1024
TILE = 128
POINTS_DEV = 1536
ITERS = 2
CLUSTERS = 4
ROWS = 12288
MAXTILES = 96
N_SHARD = 8


def draw_tile_counts(key, part):
    count_key = jax.random.fold_in(key, 11)
    place_key = jax.random.fold_in(key, 23)
    counts = jax.random.randint(count_key, (CLUSTERS,), MAXTILES // 2 + 1, MAXTILES + 1, dtype=jnp.int32)
    full_place = jax.random.randint(place_key, (), 0, CLUSTERS, dtype=jnp.int32)
    positions = jnp.arange(CLUSTERS, dtype=jnp.int32)
    return jnp.where(positions == full_place, MAXTILES, counts).astype(jnp.int32)


def block_scale(own_key, shape, split, smallest, top_value):
    def one(dim, parts):
        draws = jax.random.uniform(jax.random.fold_in(jax.random.fold_in(own_key, 6), dim), (parts,), jnp.float32, smallest / len(split), top_value / len(split))
        return jnp.repeat(jnp.exp(draws), shape[dim] // parts).reshape((-1,) + (1,) * (len(shape) - dim - 1))

    gain = one(*split[0])
    for cut in split[1:]:
        gain = gain * one(*cut)
    return gain


def bell_draw(rng, dims, spread, bound, split=(), kind=jnp.bfloat16):
    entries = jax.random.normal(rng, dims, jnp.float32) * spread
    if len(split) > 0:
        entries = block_scale(rng, dims, split, -0.22, 0.18) * entries
    return jnp.clip(entries, min=-bound, max=bound).astype(kind)


def setup_inputs(seed: int = 0) -> dict:
    key_list = jax.random.split(jax.random.key(seed), 4)
    return {
        "points": bell_draw(key_list[0], (CLUSTERS, ROWS, EMBED_WIDTH), 1.0, 6.0, ((0, 4), (1, 8))),
        "centroids": jnp.clip(jax.random.uniform(key_list[1], (CLUSTERS, K, EMBED_WIDTH), jnp.float32, -1.5, 1.5) * block_scale(key_list[1], (CLUSTERS, K, EMBED_WIDTH), ((0, 4), (1, 8)), -0.4, 0.0), -1.5, 1.5).astype(jnp.bfloat16),
        "tile_counts": draw_tile_counts(jax.random.fold_in(key_list[3], 71), 0),
    }


sharpness_factor = 48.0
epsilon = 1e-06

def rms_unit(values):
    return values * lax.rsqrt(lax.optimization_barrier(jnp.mean(values * values, axis=-1, keepdims=True)) + epsilon)

def one_cluster(clustering_arguments):
    cluster_points, start_table, tile_total = clustering_arguments
    row_index = jnp.arange(ROWS, dtype=jnp.int32)
    tile_number = row_index % POINTS_DEV // TILE * N_SHARD + row_index // POINTS_DEV
    valid_rows = (tile_number < tile_total).astype(jnp.float32)
    unit_embeddings = rms_unit(cluster_points.astype(jnp.float32)).astype(jnp.bfloat16)
    present_centroids = start_table
    updated = jnp.zeros((K, EMBED_WIDTH), jnp.float32)
    mean_rows = jnp.zeros((ROWS, EMBED_WIDTH), jnp.bfloat16)
    for iteration in range(ITERS):
        affinity_scores = lax.dot_general(unit_embeddings, present_centroids, (((1,), (1,)), ((), ())), preferred_element_type=jnp.float32) * (sharpness_factor / EMBED_WIDTH)
        exponent_terms = jnp.exp(affinity_scores)
        weights = exponent_terms / lax.optimization_barrier(jnp.sum(exponent_terms, axis=-1, keepdims=True)) * valid_rows[:, None]
        weights = weights.astype(jnp.bfloat16)
        centroid_sums = lax.dot_general(weights, unit_embeddings, (((0,), (0,)), ((), ())), preferred_element_type=jnp.float32)
        if iteration == ITERS - 1:
            mean_rows = jnp.dot(weights, present_centroids, preferred_element_type=jnp.float32).astype(jnp.bfloat16)
        updated = rms_unit(centroid_sums)
        present_centroids = updated.astype(jnp.bfloat16)
    return (updated, mean_rows)

def reference(points, centroids, tile_counts):
    new_centroids, posterior_rows = lax.map(one_cluster, (points, centroids, tile_counts))
    return (new_centroids, posterior_rows)
```

```python
import jax
import jax.numpy as jnp
from jax import lax
from jax.sharding import PartitionSpec as P

TILE = 128
ITERS = 2


sharpness_factor = 48.0
epsilon = 1e-06


def rms_unit(values):
    return values * lax.rsqrt(jnp.mean(values * values, axis=-1, keepdims=True) + epsilon)


def pick_entry(lookup_table, wanted):
    positions = jnp.arange(lookup_table.shape[0], dtype=jnp.int32)
    return jnp.sum(jnp.where(positions == wanted, lookup_table, 0))


def held_tiles(tile_total, shard_place, shard_count, slot_count):
    return jnp.clip((tile_total - shard_place + shard_count - 1) // shard_count, 0, slot_count)


def swap(values, offset):
    places = lax.axis_size("shard")
    return lax.ppermute(values, "shard", [(place, place ^ offset) for place in range(places)])


def low_bit(number):
    return number & -number


def gather_blocks(own, chips):
    held = {0: own}
    bits = [1 << b for b in range(chips.bit_length() - 1)]
    for bit in reversed(bits):
        for j in sorted(held):
            if j ^ bit not in held:
                held[j ^ bit] = swap(held[j], 2 * bit)
    return {j: (rows, swap(rows, 1)) for j, rows in held.items()}


def scatter_blocks(own_parts, other_parts, chips):
    totals = {}
    for j in sorted(own_parts, reverse=True):
        totals[j] = own_parts[j] + swap(other_parts[j].astype(jnp.bfloat16), 1).astype(jnp.float32)
    for j in sorted(totals, key=lambda j: (low_bit(j), -j)):
        if j:
            got = swap(totals[j].astype(jnp.bfloat16), 2 * low_bit(j))
            totals[j ^ low_bit(j)] = totals[j ^ low_bit(j)] + got.astype(jnp.float32)
    return totals[0]


def body(points, centroids, tile_counts):
    slot_count = points.shape[1] // TILE
    feature_width = points.shape[2]
    shard_count = lax.axis_size("shard")
    shard_place = lax.axis_index("shard")
    group_index = lax.axis_index("grp")
    chips = shard_count // 2
    unit = rms_unit(points[0].astype(jnp.float32)).astype(jnp.bfloat16)
    own_held = held_tiles(
        pick_entry(tile_counts, group_index), shard_place, shard_count, slot_count
    )
    live = (jnp.arange(slot_count * TILE) // TILE < own_held).astype(jnp.float32)
    current = centroids[0]
    count = current.shape[0]
    for iteration in range(ITERS):
        blocks = gather_blocks(current, chips)
        tables = {j: jnp.concatenate(blocks[j]) for j in blocks}
        terms = {}
        normal = 0.0
        for j in sorted(tables):
            scores = lax.dot_general(
                tables[j], unit, (((1,), (1,)), ((), ())), preferred_element_type=jnp.float32
            ) * (sharpness_factor / feature_width)
            terms[j] = jnp.exp(scores).astype(jnp.bfloat16)
            normal = normal + jnp.sum(terms[j].astype(jnp.float32), axis=0)
        factor = live / normal
        weights = {j: (terms[j].astype(jnp.float32) * factor).astype(jnp.bfloat16) for j in terms}
        sums = {j: jnp.dot(weights[j], unit, preferred_element_type=jnp.float32) for j in weights}
        reduced = scatter_blocks(
            {j: sums[j][:count] for j in sums}, {j: sums[j][count:] for j in sums}, chips
        )
        if iteration == ITERS - 1:
            out_rows = sum(
                lax.dot_general(
                    weights[j], tables[j], (((0,), (0,)), ((), ())), preferred_element_type=jnp.float32
                )
                for j in sorted(tables)
            ).astype(jnp.bfloat16)
        updated = rms_unit(reduced)
        current = updated.astype(jnp.bfloat16)
    return (updated[None], out_rows[None])


def solution(mesh):
    return jax.shard_map(
        body,
        mesh=mesh,
        in_specs=(P("grp", "shard", None), P("grp", "shard", None), P()),
        out_specs=(P("grp", "shard", None), P("grp", "shard", None)),
        check_vma=False,
    )
```

```python
import functools

import jax
import jax.numpy as jnp
from jax import lax
from jax.experimental import pallas as pl
from jax.experimental.pallas import tpu as pltpu
from jax.sharding import PartitionSpec as P

TILE = 128
ITERS = 2


sharpness_factor = 48.0
epsilon = 1e-06


def rms_unit(values):
    return values * lax.rsqrt(jnp.mean(values * values, axis=-1, keepdims=True) + epsilon)


def pick_entry(lookup_table, wanted):
    positions = jnp.arange(lookup_table.shape[0], dtype=jnp.int32)
    return jnp.sum(jnp.where(positions == wanted, lookup_table, 0))


def held_tiles(tile_total, shard_place, shard_count, slot_count):
    return jnp.clip((tile_total - shard_place + shard_count - 1) // shard_count, 0, slot_count)


def swap(values, offset):
    places = lax.axis_size("shard")
    return lax.ppermute(values, "shard", [(place, place ^ offset) for place in range(places)])


def low_bit(number):
    return number & -number


def after(values, *others):
    return lax.optimization_barrier((values, others))[0]


DIRECT_PART = 0
GDIR = 0
IN_VMEM = pl.BlockSpec(memory_space=pltpu.VMEM)
IN_SMEM = pl.BlockSpec(memory_space=pltpu.SMEM)
VMEM_ROOM = pltpu.CompilerParams(vmem_limit_bytes=24 << 20)


def cost(weight):
    return pl.CostEstimate(
        flops=weight * 2 * 256 * 1024 * 1536, bytes_accessed=5 << 20, transcendentals=0
    )


def local_call(kernel, name, outs, operands, weight=4):
    return pl.pallas_call(
        kernel,
        out_shape=outs,
        in_specs=[IN_VMEM] * len(operands),
        out_specs=[IN_VMEM] * len(outs),
        name=name,
        compiler_params=VMEM_ROOM,
        cost_estimate=cost(weight),
    )(*operands)


def live_kernel(held, out):
    place = lax.broadcasted_iota(jnp.int32, out.shape, 1)
    out[...] = (place < held[0] * TILE).astype(jnp.float32)


def live_row(held, points):
    return pl.pallas_call(
        live_kernel,
        out_shape=jax.ShapeDtypeStruct((1, points), jnp.float32),
        in_specs=[IN_SMEM],
        out_specs=IN_VMEM,
        name="live",
    )(held[None])


def scores_kernel(*refs):
    *rows, unit, terms, normal = refs
    table = jnp.concatenate([r[...] for r in rows], axis=0)
    scores = lax.dot_general(
        table, unit[...], (((1,), (1,)), ((), ())), preferred_element_type=jnp.float32
    )
    raised = jnp.exp(scores * (sharpness_factor / unit.shape[1]))
    terms[...] = raised.astype(jnp.bfloat16)
    normal[...] = jnp.sum(raised, axis=0, keepdims=True)


def scores_of(rows, unit):
    count, points = sum(r.shape[0] for r in rows), unit.shape[0]
    outs = [
        jax.ShapeDtypeStruct((count, points), jnp.bfloat16),
        jax.ShapeDtypeStruct((1, points), jnp.float32),
    ]
    return local_call(scores_kernel, "scores", outs, [*rows, unit])


def sums_kernel(terms, factor, unit, kept, given):
    half = kept.shape[0]
    weights = (terms[...].astype(jnp.float32) * factor[...]).astype(jnp.bfloat16)
    sums = jnp.dot(weights, unit[...], preferred_element_type=jnp.float32)
    kept[...] = sums[:half]
    given[...] = sums[half:].astype(jnp.bfloat16)


def sums_of(terms, factor, unit):
    shape = (terms.shape[0] // 2, unit.shape[1])
    outs = [jax.ShapeDtypeStruct(shape, t) for t in (jnp.float32, jnp.bfloat16)]
    return local_call(sums_kernel, "sums", outs, [terms, factor, unit])


def blend_kernel(blocks, *refs):
    terms, tables, factor, out = refs[:blocks], refs[blocks:-2], refs[-2], refs[-1]
    total = jnp.zeros(out.shape, jnp.float32)
    for block, table in zip(terms, tables):
        weights = (block[...].astype(jnp.float32) * factor[...]).astype(jnp.bfloat16)
        total = total + lax.dot_general(
            weights, table[...], (((0,), (0,)), ((), ())), preferred_element_type=jnp.float32
        )
    out[...] = total.astype(jnp.bfloat16)


def blend(terms, tables, factor, tile):
    blocks, points = len(terms), factor.shape[1]
    tables = [jnp.concatenate(t) for t in tables]
    width = tables[0].shape[1]
    return pl.pallas_call(
        functools.partial(blend_kernel, blocks),
        grid=(points // tile,),
        out_shape=jax.ShapeDtypeStruct((points, width), jnp.bfloat16),
        in_specs=[pl.BlockSpec((t.shape[0], tile), lambda i: (0, i)) for t in terms]
        + [pl.BlockSpec(t.shape, lambda i: (0, 0)) for t in tables]
        + [pl.BlockSpec((1, tile), lambda i: (0, i))],
        out_specs=pl.BlockSpec((tile, width), lambda i: (i, 0)),
        name="blend",
        compiler_params=VMEM_ROOM,
        cost_estimate=cost(16),
    )(*terms, *tables, factor)


def bits_of(chips):
    return [1 << b for b in range(chips.bit_length() - 1)]


def direct_rows(count):
    return count // DIRECT_PART // 16 * 16 if DIRECT_PART else 0


def gather_terms(own, unit, chips):
    bits, cut = bits_of(chips), GDIR and direct_rows(own.shape[0])
    beside = swap(own, 1)
    near = swap(own, 2)
    stepped = {0: own[cut:]}
    for bit in reversed(bits):
        for j in sorted(stepped):
            if j ^ bit not in stepped and j ^ bit != 1:
                stepped[j ^ bit] = swap(stepped[j], 2 * bit)
    rows = {0: [own], 1: [near]}
    for j in range(2, chips):
        straight = [swap(after(own[:cut], beside), 2 * j)] if cut else []
        rows[j] = [*straight, stepped[j]]
    tables, terms = {}, {}
    for j in range(chips):
        if j:
            held = after(rows[j][-1], *terms.values()) if j == chips - 1 else rows[j][-1]
            others = [swap(r, 1) for r in (*rows[j][:-1], held)]
        else:
            others = [beside]
        tables[j] = [*rows[j], *others]
        terms[j] = scores_of(tables[j], unit)
    return tables, terms


def scatter_sums(terms, factor, unit, chips, beside):
    bits = bits_of(chips)
    order = sorted(terms, key=lambda j: (low_bit(j) or chips, -j))
    kept, given, totals, gate = {}, {}, {}, ()
    for place, j in enumerate(order):
        kept[j], given[j] = sums_of(after(terms[j], *gate), factor, unit)
        if j:
            totals[j] = kept[j] + swap(given[j], 1).astype(jnp.float32)
        gate = (totals[order[0]],) if place else (given[j],)
    cut = direct_rows(kept[0].shape[0])
    straight = []
    stepped = {j: totals[j][cut:] for j in totals if j > 1}
    for j in order:
        if j > 1:
            bit = low_bit(j)
            if cut:
                straight.append(swap(totals[j][:cut].astype(jnp.bfloat16), 2 * j))
            gate = stepped[j]
            got = swap(stepped[j].astype(jnp.bfloat16), 2 * bit).astype(jnp.float32)
            stepped[j ^ bit] = stepped[j ^ bit] + got if j ^ bit else got
    near = swap(after(totals[1].astype(jnp.bfloat16), given[0]), 2)
    done = beside(gate)
    mine = kept[0] + swap(after(given[0], *done), 1).astype(jnp.float32) + near.astype(jnp.float32)
    far = stepped[0]
    if cut:
        far = jnp.concatenate([sum(s.astype(jnp.float32) for s in straight), far])
    return mine + far, done


def body(points, centroids, tile_counts):
    slot_count = points.shape[1] // TILE
    shard_count = lax.axis_size("shard")
    shard_place = lax.axis_index("shard")
    group_index = lax.axis_index("grp")
    chips = shard_count // 2
    own_held = held_tiles(
        pick_entry(tile_counts, group_index), shard_place, shard_count, slot_count
    )
    live = live_row(own_held, slot_count * TILE)
    unit = rms_unit(after(points[0], live).astype(jnp.float32)).astype(jnp.bfloat16)
    current = centroids[0]
    for iteration in range(ITERS):
        tables, scored = gather_terms(current, unit, chips)
        terms = {j: scored[j][0] for j in scored}
        factor = live / sum(scored[j][1] for j in sorted(scored))

        def posterior(gate):
            if iteration < ITERS - 1:
                return ()
            blocks = sorted(tables)
            return (
                blend([after(terms[j], gate) for j in blocks], [tables[j] for j in blocks], factor, 2 * TILE),
            )

        reduced, out_rows = scatter_sums(terms, factor, unit, chips, posterior)
        updated = rms_unit(reduced)
        current = updated.astype(jnp.bfloat16)
    return (updated[None], out_rows[0][None])


def solution(mesh):
    return jax.shard_map(
        body,
        mesh=mesh,
        in_specs=(P("grp", "shard", None), P("grp", "shard", None), P()),
        out_specs=(P("grp", "shard", None), P("grp", "shard", None)),
        check_vma=False,
    )
```

```python
import functools

import jax
import jax.numpy as jnp
from jax import lax
from jax.experimental import pallas as pl
from jax.experimental.pallas import tpu as pltpu
from jax.sharding import PartitionSpec as P

TILE = 128
ITERS = 2


sharpness_factor = 48.0
epsilon = 1e-06


def rms_unit(values):
    return values * lax.rsqrt(jnp.mean(values * values, axis=-1, keepdims=True) + epsilon)


def pick_entry(lookup_table, wanted):
    positions = jnp.arange(lookup_table.shape[0], dtype=jnp.int32)
    return jnp.sum(jnp.where(positions == wanted, lookup_table, 0))


def held_tiles(tile_total, shard_place, shard_count, slot_count):
    return jnp.clip((tile_total - shard_place + shard_count - 1) // shard_count, 0, slot_count)


def swap(values, offset):
    places = lax.axis_size("shard")
    return lax.ppermute(values, "shard", [(place, place ^ offset) for place in range(places)])


def after(values, *others):
    return lax.optimization_barrier((values, others))[0]


IN_VMEM = pl.BlockSpec(memory_space=pltpu.VMEM)
IN_SMEM = pl.BlockSpec(memory_space=pltpu.SMEM)
VMEM_ROOM = pltpu.CompilerParams(vmem_limit_bytes=24 << 20)


def cost(weight):
    return pl.CostEstimate(
        flops=weight * 2 * 256 * 1024 * 1536, bytes_accessed=5 << 20, transcendentals=0
    )


def local_call(kernel, name, outs, operands, weight=4):
    return pl.pallas_call(
        kernel,
        out_shape=outs,
        in_specs=[IN_VMEM] * len(operands),
        out_specs=[IN_VMEM] * len(outs),
        name=name,
        compiler_params=VMEM_ROOM,
        cost_estimate=cost(weight),
    )(*operands)


def live_kernel(held, out):
    place = lax.broadcasted_iota(jnp.int32, out.shape, 1)
    out[...] = (place < held[0] * TILE).astype(jnp.float32)


def live_row(held, points):
    return pl.pallas_call(
        live_kernel,
        out_shape=jax.ShapeDtypeStruct((1, points), jnp.float32),
        in_specs=[IN_SMEM],
        out_specs=IN_VMEM,
        name="live",
    )(held[None])


def scores_kernel(*refs):
    *rows, unit, terms, normal = refs
    table = jnp.concatenate([r[...] for r in rows], axis=0)
    scores = lax.dot_general(
        table, unit[...], (((1,), (1,)), ((), ())), preferred_element_type=jnp.float32
    )
    raised = jnp.exp(scores * (sharpness_factor / unit.shape[1]))
    terms[...] = raised.astype(jnp.bfloat16)
    normal[...] = jnp.sum(raised, axis=0, keepdims=True)


def scores_of(rows, unit):
    count, points = sum(r.shape[0] for r in rows), unit.shape[0]
    outs = [
        jax.ShapeDtypeStruct((count, points), jnp.bfloat16),
        jax.ShapeDtypeStruct((1, points), jnp.float32),
    ]
    return local_call(scores_kernel, "scores", outs, [*rows, unit])


def sums_kernel(terms, factor, unit, kept, given):
    half = kept.shape[0]
    weights = (terms[...].astype(jnp.float32) * factor[...]).astype(jnp.bfloat16)
    sums = jnp.dot(weights, unit[...], preferred_element_type=jnp.float32)
    kept[...] = sums[:half]
    given[...] = sums[half:].astype(jnp.bfloat16)


def sums_of(terms, factor, unit):
    shape = (terms.shape[0] // 2, unit.shape[1])
    outs = [jax.ShapeDtypeStruct(shape, t) for t in (jnp.float32, jnp.bfloat16)]
    return local_call(sums_kernel, "sums", outs, [terms, factor, unit])


def blend_kernel(blocks, *refs):
    terms, tables, factor, out = refs[:blocks], refs[blocks:-2], refs[-2], refs[-1]
    total = jnp.zeros(out.shape, jnp.float32)
    for block, table in zip(terms, tables):
        weights = (block[...].astype(jnp.float32) * factor[...]).astype(jnp.bfloat16)
        total = total + lax.dot_general(
            weights, table[...], (((0,), (0,)), ((), ())), preferred_element_type=jnp.float32
        )
    out[...] = total.astype(jnp.bfloat16)


def blend(terms, tables, factor, tile):
    blocks, points = len(terms), factor.shape[1]
    tables = [jnp.concatenate(t) for t in tables]
    width = tables[0].shape[1]
    return pl.pallas_call(
        functools.partial(blend_kernel, blocks),
        grid=(points // tile,),
        out_shape=jax.ShapeDtypeStruct((points, width), jnp.bfloat16),
        in_specs=[pl.BlockSpec((t.shape[0], tile), lambda i: (0, i)) for t in terms]
        + [pl.BlockSpec(t.shape, lambda i: (0, 0)) for t in tables]
        + [pl.BlockSpec((1, tile), lambda i: (0, i))],
        out_specs=pl.BlockSpec((tile, width), lambda i: (i, 0)),
        name="blend",
        compiler_params=VMEM_ROOM,
        cost_estimate=cost(16),
    )(*terms, *tables, factor)


def low_bit(number):
    return number & -number


def offset(j):
    return j ^ (j >> 1) ^ (j >> 2) ^ (j >> 3) ^ (j >> 4)


def step(values, j):
    return swap(values, 2 * offset(j))


def bits_of(chips):
    return [1 << b for b in range(chips.bit_length() - 1)]


def gather_terms(own, unit, chips):
    rows = {0: own}
    for bit in reversed(bits_of(chips)):
        for j in sorted(rows):
            rows[j ^ bit] = step(rows[j], bit)
    tables, terms = {}, {}
    for j in range(chips):
        held = after(rows[j], *terms.values()) if j == chips - 1 else rows[j]
        tables[j] = [rows[j], swap(held, 1)]
        terms[j] = scores_of(tables[j], unit)
    return tables, terms


def scatter_sums(terms, factor, unit, chips, beside):
    order = sorted(terms, key=lambda j: (low_bit(j) or chips, -j))
    kept, given, totals, gate = {}, {}, {}, ()
    for place, j in enumerate(order):
        kept[j], given[j] = sums_of(after(terms[j], *gate), factor, unit)
        if j:
            totals[j] = kept[j] + swap(given[j], 1).astype(jnp.float32)
        gate = (totals[order[0]],) if place else (given[j],)
    got = {}
    for j in order:
        if j > 1:
            bit, gate = low_bit(j), totals[j]
            got[j] = step(totals[j].astype(jnp.bfloat16), bit).astype(jnp.float32)
            if j ^ bit:
                totals[j ^ bit] = totals[j ^ bit] + got.pop(j)
    near = step(after(totals[1].astype(jnp.bfloat16), given[0]), 1).astype(jnp.float32)
    done = beside(gate)
    mine = kept[0] + swap(after(given[0], *done), 1).astype(jnp.float32) + near
    return mine + sum(got.values()), done


def body(points, centroids, tile_counts):
    slot_count = points.shape[1] // TILE
    shard_count = lax.axis_size("shard")
    shard_place = lax.axis_index("shard")
    group_index = lax.axis_index("grp")
    chips = shard_count // 2
    own_held = held_tiles(
        pick_entry(tile_counts, group_index), shard_place, shard_count, slot_count
    )
    live = live_row(own_held, slot_count * TILE)
    unit = rms_unit(after(points[0], live).astype(jnp.float32)).astype(jnp.bfloat16)
    current = centroids[0]
    for iteration in range(ITERS):
        tables, scored = gather_terms(current, unit, chips)
        terms = {j: scored[j][0] for j in scored}
        factor = live / sum(scored[j][1] for j in sorted(scored))

        def posterior(gate):
            if iteration < ITERS - 1:
                return ()
            blocks = sorted(tables)
            return (
                blend([after(terms[j], gate) for j in blocks], [tables[j] for j in blocks], factor, 2 * TILE),
            )

        reduced, out_rows = scatter_sums(terms, factor, unit, chips, posterior)
        updated = rms_unit(reduced)
        current = updated.astype(jnp.bfloat16)
    return (updated[None], out_rows[0][None])


def solution(mesh):
    return jax.shard_map(
        body,
        mesh=mesh,
        in_specs=(P("grp", "shard", None), P("grp", "shard", None), P()),
        out_specs=(P("grp", "shard", None), P("grp", "shard", None)),
        check_vma=False,
    )
```

```python
import functools

import jax
import jax.numpy as jnp
from jax import lax
from jax.experimental import pallas as pl
from jax.experimental.pallas import tpu as pltpu
from jax.sharding import PartitionSpec as P

TILE = 128
ITERS = 2


sharpness_factor = 48.0
epsilon = 1e-06


def rms_unit(values):
    return values * lax.rsqrt(jnp.mean(values * values, axis=-1, keepdims=True) + epsilon)


def pick_entry(lookup_table, wanted):
    positions = jnp.arange(lookup_table.shape[0], dtype=jnp.int32)
    return jnp.sum(jnp.where(positions == wanted, lookup_table, 0))


def held_tiles(tile_total, shard_place, shard_count, slot_count):
    return jnp.clip((tile_total - shard_place + shard_count - 1) // shard_count, 0, slot_count)


def swap(values, offset):
    places = lax.axis_size("shard")
    return lax.ppermute(values, "shard", [(place, place ^ offset) for place in range(places)])


def after(values, *others):
    return lax.optimization_barrier((values, others))[0]


IN_VMEM = pl.BlockSpec(memory_space=pltpu.VMEM)
IN_SMEM = pl.BlockSpec(memory_space=pltpu.SMEM)
VMEM_ROOM = pltpu.CompilerParams(vmem_limit_bytes=24 << 20)


def cost(weight):
    return pl.CostEstimate(
        flops=weight * 2 * 256 * 1024 * 1536, bytes_accessed=5 << 20, transcendentals=0
    )


def local_call(kernel, name, outs, operands, weight=4):
    return pl.pallas_call(
        kernel,
        out_shape=outs,
        in_specs=[IN_VMEM] * len(operands),
        out_specs=[IN_VMEM] * len(outs),
        name=name,
        compiler_params=VMEM_ROOM,
        cost_estimate=cost(weight),
    )(*operands)


def live_kernel(held, out):
    place = lax.broadcasted_iota(jnp.int32, out.shape, 1)
    out[...] = (place < held[0] * TILE).astype(jnp.float32)


def live_row(held, points):
    return pl.pallas_call(
        live_kernel,
        out_shape=jax.ShapeDtypeStruct((1, points), jnp.float32),
        in_specs=[IN_SMEM],
        out_specs=IN_VMEM,
        name="live",
    )(held[None])


def scores_kernel(*refs):
    *rows, unit, terms, normal = refs
    table = jnp.concatenate([r[...] for r in rows], axis=0)
    scores = lax.dot_general(
        table, unit[...], (((1,), (1,)), ((), ())), preferred_element_type=jnp.float32
    )
    raised = jnp.exp(scores * (sharpness_factor / unit.shape[1]))
    terms[...] = raised
    normal[...] = jnp.sum(raised, axis=0, keepdims=True)


def scores_of(rows, unit):
    count, points = sum(r.shape[0] for r in rows), unit.shape[0]
    outs = [
        jax.ShapeDtypeStruct((count, points), jnp.float32),
        jax.ShapeDtypeStruct((1, points), jnp.float32),
    ]
    return local_call(scores_kernel, "scores", outs, [*rows, unit])


def sums_kernel(terms, factor, unit, kept, given):
    half = kept.shape[0]
    weights = (terms[...] * factor[...]).astype(jnp.bfloat16)
    sums = jnp.dot(weights, unit[...], preferred_element_type=jnp.float32)
    kept[...] = sums[:half]
    given[...] = sums[half:].astype(jnp.bfloat16)


def sums_of(terms, factor, unit):
    shape = (terms.shape[0] // 2, unit.shape[1])
    outs = [jax.ShapeDtypeStruct(shape, t) for t in (jnp.float32, jnp.bfloat16)]
    return local_call(sums_kernel, "sums", outs, [terms, factor, unit])


def last_kernel(blocks, own_rows, other_rows, unit, live, *refs):
    *refs, factor, kept, given = refs
    normals, kept_terms = refs[:blocks], refs[blocks:]
    half = kept.shape[0]
    table = jnp.concatenate([own_rows[...], other_rows[...]], axis=0)
    scores = lax.dot_general(
        table, unit[...], (((1,), (1,)), ((), ())), preferred_element_type=jnp.float32
    )
    raised = jnp.exp(scores * (sharpness_factor / unit.shape[1]))
    for terms in kept_terms:
        terms[...] = raised
    normal = jnp.sum(raised, axis=0, keepdims=True) + sum(n[...] for n in normals)
    scale = live[...] / normal
    factor[...] = scale
    sums = jnp.dot((raised * scale).astype(jnp.bfloat16), unit[...], preferred_element_type=jnp.float32)
    kept[...] = sums[:half]
    given[...] = sums[half:].astype(jnp.bfloat16)


def last_block(rows, unit, live, normals, with_terms):
    own, points = rows[0].shape, unit.shape[0]
    outs = [jax.ShapeDtypeStruct((2 * own[0], points), jnp.float32)] * with_terms + [
        jax.ShapeDtypeStruct((1, points), jnp.float32),
        jax.ShapeDtypeStruct(own, jnp.float32),
        jax.ShapeDtypeStruct(own, jnp.bfloat16),
    ]
    kernel = functools.partial(last_kernel, len(normals))
    return local_call(kernel, "last", outs, [*rows, unit, live, *normals], 4)


def blend_kernel(blocks, *refs):
    terms, tables, factor, out = refs[:blocks], refs[blocks:-2], refs[-2], refs[-1]
    total = jnp.zeros(out.shape, jnp.float32)
    for block, table in zip(terms, tables):
        weights = (block[...] * factor[...]).astype(jnp.bfloat16)
        total = total + lax.dot_general(
            weights, table[...], (((0,), (0,)), ((), ())), preferred_element_type=jnp.float32
        )
    out[...] = total.astype(jnp.bfloat16)


def blend(terms, tables, factor, tile):
    blocks, points = len(terms), factor.shape[1]
    tables = [jnp.concatenate(t) for t in tables]
    width = tables[0].shape[1]
    return pl.pallas_call(
        functools.partial(blend_kernel, blocks),
        grid=(points // tile,),
        out_shape=jax.ShapeDtypeStruct((points, width), jnp.bfloat16),
        in_specs=[pl.BlockSpec((t.shape[0], tile), lambda i: (0, i)) for t in terms]
        + [pl.BlockSpec(t.shape, lambda i: (0, 0)) for t in tables]
        + [pl.BlockSpec((1, tile), lambda i: (0, i))],
        out_specs=pl.BlockSpec((tile, width), lambda i: (i, 0)),
        name="blend",
        compiler_params=VMEM_ROOM,
        cost_estimate=cost(16),
    )(*terms, *tables, factor)


def low_bit(number):
    return number & -number


def offset(j):
    return j ^ (j >> 1) ^ (j >> 2) ^ (j >> 3) ^ (j >> 4)


def step(values, j):
    return swap(values, 2 * offset(j))


def bits_of(chips):
    return [1 << b for b in range(chips.bit_length() - 1)]


def gather_terms(own, unit, chips):
    rows = {0: own}
    for bit in reversed(bits_of(chips)):
        for j in sorted(rows):
            rows[j ^ bit] = step(rows[j], bit)
    tables, terms = {}, {}
    for j in range(chips):
        held = after(rows[j], *terms.values()) if j == chips - 1 else rows[j]
        tables[j] = [rows[j], swap(held, 1)]
        if j < chips - 1:
            terms[j] = scores_of(tables[j], unit)
    return tables, terms


def scatter_sums(terms, factor, first, unit, chips, beside):
    order = sorted(range(chips), key=lambda j: (low_bit(j) or chips, -j))
    kept, given, totals, gate = {}, {}, {}, ()
    for place, j in enumerate(order):
        if place:
            kept[j], given[j] = sums_of(after(terms[j], *gate), factor, unit)
        else:
            kept[j], given[j] = first
        if j:
            totals[j] = kept[j] + swap(given[j], 1).astype(jnp.float32)
        gate = (totals[order[0]],) if place else (given[j],)
    got = {}
    for j in order:
        if j > 1:
            bit, gate = low_bit(j), totals[j]
            got[j] = step(totals[j].astype(jnp.bfloat16), bit).astype(jnp.float32)
            if j ^ bit:
                totals[j ^ bit] = totals[j ^ bit] + got.pop(j)
    near = step(after(totals[1].astype(jnp.bfloat16), given[0]), 1).astype(jnp.float32)
    done = beside(gate)
    mine = kept[0] + swap(after(given[0], *done), 1).astype(jnp.float32) + near
    return mine + sum(got.values()), done


def body(points, centroids, tile_counts):
    slot_count = points.shape[1] // TILE
    shard_count = lax.axis_size("shard")
    shard_place = lax.axis_index("shard")
    group_index = lax.axis_index("grp")
    chips = shard_count // 2
    own_held = held_tiles(
        pick_entry(tile_counts, group_index), shard_place, shard_count, slot_count
    )
    live = live_row(own_held, slot_count * TILE)
    unit = rms_unit(after(points[0], live).astype(jnp.float32)).astype(jnp.bfloat16)
    current = centroids[0]
    for iteration in range(ITERS):
        tables, scored = gather_terms(current, unit, chips)
        terms = {j: scored[j][0] for j in scored}
        normals = [scored[j][1] for j in sorted(scored)]
        is_last = iteration == ITERS - 1
        *kept_terms, factor, kept, given = last_block(tables[chips - 1], unit, live, normals, is_last)
        if is_last:
            terms[chips - 1] = kept_terms[0]

        def posterior(gate):
            if not is_last:
                return ()
            blocks = sorted(tables)
            return (
                blend([after(terms[j], gate) for j in blocks], [tables[j] for j in blocks], factor, 2 * TILE),
            )

        reduced, out_rows = scatter_sums(terms, factor, (kept, given), unit, chips, posterior)
        updated = rms_unit(reduced)
        current = updated.astype(jnp.bfloat16)
    return (updated[None], out_rows[0][None])


def solution(mesh):
    return jax.shard_map(
        body,
        mesh=mesh,
        in_specs=(P("grp", "shard", None), P("grp", "shard", None), P()),
        out_specs=(P("grp", "shard", None), P("grp", "shard", None)),
        check_vma=False,
    )
```

```python
import functools

import jax
import jax.numpy as jnp
from jax import lax
from jax.experimental import pallas as pl
from jax.experimental.pallas import tpu as pltpu
from jax.sharding import PartitionSpec as P

TILE = 128
ITERS = 2


sharpness_factor = 48.0
epsilon = 1e-06


def rms_unit(values):
    return values * lax.rsqrt(jnp.mean(values * values, axis=-1, keepdims=True) + epsilon)


def pick_entry(lookup_table, wanted):
    positions = jnp.arange(lookup_table.shape[0], dtype=jnp.int32)
    return jnp.sum(jnp.where(positions == wanted, lookup_table, 0))


def held_tiles(tile_total, shard_place, shard_count, slot_count):
    return jnp.clip((tile_total - shard_place + shard_count - 1) // shard_count, 0, slot_count)


def swap(values, offset):
    places = lax.axis_size("shard")
    return lax.ppermute(values, "shard", [(place, place ^ offset) for place in range(places)])


def after(values, *others):
    return lax.optimization_barrier((values, others))[0]


IN_VMEM = pl.BlockSpec(memory_space=pltpu.VMEM)
IN_SMEM = pl.BlockSpec(memory_space=pltpu.SMEM)
VMEM_ROOM = pltpu.CompilerParams(vmem_limit_bytes=24 << 20)


def cost(weight):
    return pl.CostEstimate(
        flops=weight * 2 * 256 * 1024 * 1536, bytes_accessed=5 << 20, transcendentals=0
    )


def local_call(kernel, name, outs, operands, weight=4):
    return pl.pallas_call(
        kernel,
        out_shape=outs,
        in_specs=[IN_VMEM] * len(operands),
        out_specs=[IN_VMEM] * len(outs),
        name=name,
        compiler_params=VMEM_ROOM,
        cost_estimate=cost(weight),
    )(*operands)


def live_kernel(held, out):
    place = lax.broadcasted_iota(jnp.int32, out.shape, 1)
    out[...] = (place < held[0] * TILE).astype(jnp.float32)


def live_row(held, points):
    return pl.pallas_call(
        live_kernel,
        out_shape=jax.ShapeDtypeStruct((1, points), jnp.float32),
        in_specs=[IN_SMEM],
        out_specs=IN_VMEM,
        name="live",
    )(held[None])


def scores_kernel(*refs):
    *rows, unit, terms, normal = refs
    table = jnp.concatenate([r[...] for r in rows], axis=0)
    scores = lax.dot_general(
        table, unit[...], (((1,), (1,)), ((), ())), preferred_element_type=jnp.float32
    )
    raised = jnp.exp(scores * (sharpness_factor / unit.shape[1]))
    terms[...] = raised
    normal[...] = jnp.sum(raised, axis=0, keepdims=True)


def scores_of(rows, unit):
    count, points = sum(r.shape[0] for r in rows), unit.shape[0]
    outs = [
        jax.ShapeDtypeStruct((count, points), jnp.float32),
        jax.ShapeDtypeStruct((1, points), jnp.float32),
    ]
    return local_call(scores_kernel, "scores", outs, [*rows, unit])


def sums_kernel(terms, factor, unit, kept, given):
    half = kept.shape[0]
    weights = (terms[...] * factor[...]).astype(jnp.bfloat16)
    sums = jnp.dot(weights, unit[...], preferred_element_type=jnp.float32)
    kept[...] = sums[:half]
    given[...] = sums[half:].astype(jnp.bfloat16)


def sums_of(terms, factor, unit):
    shape = (terms.shape[0] // 2, unit.shape[1])
    outs = [jax.ShapeDtypeStruct(shape, t) for t in (jnp.float32, jnp.bfloat16)]
    return local_call(sums_kernel, "sums", outs, [terms, factor, unit])


def last_kernel(blocks, own_rows, other_rows, unit, live, *refs):
    *refs, factor, kept, given = refs
    normals, kept_terms = refs[:blocks], refs[blocks:]
    half = kept.shape[0]
    table = jnp.concatenate([own_rows[...], other_rows[...]], axis=0)
    scores = lax.dot_general(
        table, unit[...], (((1,), (1,)), ((), ())), preferred_element_type=jnp.float32
    )
    raised = jnp.exp(scores * (sharpness_factor / unit.shape[1]))
    for terms in kept_terms:
        terms[...] = raised
    normal = jnp.sum(raised, axis=0, keepdims=True) + sum(n[...] for n in normals)
    scale = live[...] / normal
    factor[...] = scale
    sums = jnp.dot((raised * scale).astype(jnp.bfloat16), unit[...], preferred_element_type=jnp.float32)
    kept[...] = sums[:half]
    given[...] = sums[half:].astype(jnp.bfloat16)


def last_block(rows, unit, live, normals, with_terms):
    own, points = rows[0].shape, unit.shape[0]
    outs = [jax.ShapeDtypeStruct((2 * own[0], points), jnp.float32)] * with_terms + [
        jax.ShapeDtypeStruct((1, points), jnp.float32),
        jax.ShapeDtypeStruct(own, jnp.float32),
        jax.ShapeDtypeStruct(own, jnp.bfloat16),
    ]
    kernel = functools.partial(last_kernel, len(normals))
    return local_call(kernel, "last", outs, [*rows, unit, live, *normals], 4)


def blend_kernel(blocks, *refs):
    terms, tables, factor, out = refs[:blocks], refs[blocks:-2], refs[-2], refs[-1]
    total = jnp.zeros(out.shape, jnp.float32)
    for block, table in zip(terms, tables):
        weights = (block[...] * factor[...]).astype(jnp.bfloat16)
        total = total + lax.dot_general(
            weights, table[...], (((0,), (0,)), ((), ())), preferred_element_type=jnp.float32
        )
    out[...] = total.astype(jnp.bfloat16)


def blend(terms, tables, factor, tile):
    blocks, points = len(terms), factor.shape[1]
    tables = [jnp.concatenate(t) for t in tables]
    width = tables[0].shape[1]
    return pl.pallas_call(
        functools.partial(blend_kernel, blocks),
        grid=(points // tile,),
        out_shape=jax.ShapeDtypeStruct((points, width), jnp.bfloat16),
        in_specs=[pl.BlockSpec((t.shape[0], tile), lambda i: (0, i)) for t in terms]
        + [pl.BlockSpec(t.shape, lambda i: (0, 0)) for t in tables]
        + [pl.BlockSpec((1, tile), lambda i: (0, i))],
        out_specs=pl.BlockSpec((tile, width), lambda i: (i, 0)),
        name="blend",
        compiler_params=VMEM_ROOM,
        cost_estimate=cost(16),
    )(*terms, *tables, factor)


def low_bit(number):
    return number & -number


def offset(j):
    return j ^ (j >> 1) ^ (j >> 2) ^ (j >> 3) ^ (j >> 4)


def step(values, j):
    return swap(values, 2 * offset(j))


def bits_of(chips):
    return [1 << b for b in range(chips.bit_length() - 1)]


def gather_terms(own, unit, chips):
    rows = {0: own}
    for bit in reversed(bits_of(chips)):
        for j in sorted(rows):
            rows[j ^ bit] = step(rows[j], bit)
    tables, terms = {}, {}
    for j in range(chips):
        held = after(rows[j], *terms.values()) if j == chips - 1 else rows[j]
        tables[j] = [rows[j], swap(held, 1)]
        if j < chips - 1:
            terms[j] = scores_of(tables[j], unit)
    return tables, terms


def scatter_sums(terms, factor, first, unit, chips, beside):
    order = sorted(range(chips), key=lambda j: (low_bit(j) or chips, -j))
    kept, given, totals, gate = {}, {}, {}, ()
    for place, j in enumerate(order):
        if place:
            kept[j], given[j] = sums_of(after(terms[j], *gate), factor, unit)
        else:
            kept[j], given[j] = first
        if j:
            totals[j] = kept[j] + swap(after(given[j], *totals.values()), 1).astype(jnp.float32)
        gate = (totals[order[0]],) if place else (given[j],)
    got = {}
    for j in order:
        if j > 1:
            bit, gate = low_bit(j), totals[j]
            got[j] = step(totals[j].astype(jnp.bfloat16), bit).astype(jnp.float32)
            if j ^ bit:
                totals[j ^ bit] = totals[j ^ bit] + got.pop(j)
    near = step(after(totals[1].astype(jnp.bfloat16), given[0]), 1).astype(jnp.float32)
    done = beside(gate)
    mine = kept[0] + swap(after(given[0], *done), 1).astype(jnp.float32) + near
    return mine + sum(got.values()), done


def body(points, centroids, tile_counts):
    slot_count = points.shape[1] // TILE
    shard_count = lax.axis_size("shard")
    shard_place = lax.axis_index("shard")
    group_index = lax.axis_index("grp")
    chips = shard_count // 2
    own_held = held_tiles(
        pick_entry(tile_counts, group_index), shard_place, shard_count, slot_count
    )
    live = live_row(own_held, slot_count * TILE)
    unit = rms_unit(after(points[0], live).astype(jnp.float32)).astype(jnp.bfloat16)
    current = centroids[0]
    for iteration in range(ITERS):
        tables, scored = gather_terms(current, unit, chips)
        terms = {j: scored[j][0] for j in scored}
        normals = [scored[j][1] for j in sorted(scored)]
        is_last = iteration == ITERS - 1
        *kept_terms, factor, kept, given = last_block(tables[chips - 1], unit, live, normals, is_last)
        if is_last:
            terms[chips - 1] = kept_terms[0]

        def posterior(gate):
            if not is_last:
                return ()
            blocks = sorted(tables)
            return (
                blend([after(terms[j], gate) for j in blocks], [tables[j] for j in blocks], factor, 2 * TILE),
            )

        reduced, out_rows = scatter_sums(terms, factor, (kept, given), unit, chips, posterior)
        updated = rms_unit(reduced)
        current = updated.astype(jnp.bfloat16)
    return (updated[None], out_rows[0][None])


def solution(mesh):
    return jax.shard_map(
        body,
        mesh=mesh,
        in_specs=(P("grp", "shard", None), P("grp", "shard", None), P()),
        out_specs=(P("grp", "shard", None), P("grp", "shard", None)),
        check_vma=False,
    )
```

```python
import functools

import jax
import jax.numpy as jnp
from jax import lax
from jax.experimental import pallas as pl
from jax.experimental.pallas import tpu as pltpu
from jax.sharding import PartitionSpec as P

TILE = 128
ITERS = 2


sharpness_factor = 48.0
epsilon = 1e-06
LOG2_E = 1.4426950408889634


def rms_unit(values):
    return values * lax.rsqrt(jnp.mean(values * values, axis=-1, keepdims=True) + epsilon)


def pick_entry(lookup_table, wanted):
    positions = jnp.arange(lookup_table.shape[0], dtype=jnp.int32)
    return jnp.sum(jnp.where(positions == wanted, lookup_table, 0))


def held_tiles(tile_total, shard_place, shard_count, slot_count):
    return jnp.clip((tile_total - shard_place + shard_count - 1) // shard_count, 0, slot_count)


def swap(values, offset):
    places = lax.axis_size("shard")
    return lax.ppermute(values, "shard", [(place, place ^ offset) for place in range(places)])


def after(values, *others):
    return lax.optimization_barrier((values, others))[0]


IN_VMEM = pl.BlockSpec(memory_space=pltpu.VMEM)
IN_SMEM = pl.BlockSpec(memory_space=pltpu.SMEM)
VMEM_ROOM = pltpu.CompilerParams(vmem_limit_bytes=24 << 20)


def cost(weight):
    return pl.CostEstimate(
        flops=weight * 2 * 256 * 1024 * 1536, bytes_accessed=5 << 20, transcendentals=0
    )


def local_call(kernel, name, outs, operands, weight=4):
    return pl.pallas_call(
        kernel,
        out_shape=outs,
        in_specs=[IN_VMEM] * len(operands),
        out_specs=[IN_VMEM] * len(outs),
        name=name,
        compiler_params=VMEM_ROOM,
        cost_estimate=cost(weight),
    )(*operands)


def live_kernel(held, out):
    place = lax.broadcasted_iota(jnp.int32, out.shape, 1)
    out[...] = (place < held[0] * TILE).astype(jnp.float32)


def live_row(held, points):
    return pl.pallas_call(
        live_kernel,
        out_shape=jax.ShapeDtypeStruct((1, points), jnp.float32),
        in_specs=[IN_SMEM],
        out_specs=IN_VMEM,
        name="live",
    )(held[None])


def scores_kernel(*refs):
    *rows, unit, terms, normal = refs
    table = jnp.concatenate([r[...] for r in rows], axis=0)
    scores = lax.dot_general(
        table, unit[...], (((1,), (1,)), ((), ())), preferred_element_type=jnp.float32
    )
    raised = jnp.exp2(scores * (sharpness_factor * LOG2_E / unit.shape[1]))
    terms[...] = raised
    normal[...] = jnp.sum(raised, axis=0, keepdims=True)


def scores_of(rows, unit):
    count, points = sum(r.shape[0] for r in rows), unit.shape[0]
    outs = [
        jax.ShapeDtypeStruct((count, points), jnp.float32),
        jax.ShapeDtypeStruct((1, points), jnp.float32),
    ]
    return local_call(scores_kernel, "scores", outs, [*rows, unit])


def sums_kernel(terms, factor, unit, kept, given):
    half = kept.shape[0]
    weights = (terms[...] * factor[...]).astype(jnp.bfloat16)
    sums = jnp.dot(weights, unit[...], preferred_element_type=jnp.float32)
    kept[...] = sums[:half]
    given[...] = sums[half:].astype(jnp.bfloat16)


def sums_of(terms, factor, unit):
    shape = (terms.shape[0] // 2, unit.shape[1])
    outs = [jax.ShapeDtypeStruct(shape, t) for t in (jnp.float32, jnp.bfloat16)]
    return local_call(sums_kernel, "sums", outs, [terms, factor, unit])


def last_kernel(blocks, own_rows, other_rows, unit, live, *refs):
    *refs, factor, kept, given = refs
    normals, kept_terms = refs[:blocks], refs[blocks:]
    half = kept.shape[0]
    table = jnp.concatenate([own_rows[...], other_rows[...]], axis=0)
    scores = lax.dot_general(
        table, unit[...], (((1,), (1,)), ((), ())), preferred_element_type=jnp.float32
    )
    raised = jnp.exp2(scores * (sharpness_factor * LOG2_E / unit.shape[1]))
    for terms in kept_terms:
        terms[...] = raised
    normal = jnp.sum(raised, axis=0, keepdims=True) + sum(n[...] for n in normals)
    scale = live[...] / normal
    factor[...] = scale
    sums = jnp.dot((raised * scale).astype(jnp.bfloat16), unit[...], preferred_element_type=jnp.float32)
    kept[...] = sums[:half]
    given[...] = sums[half:].astype(jnp.bfloat16)


def last_block(rows, unit, live, normals, with_terms):
    own, points = rows[0].shape, unit.shape[0]
    outs = [jax.ShapeDtypeStruct((2 * own[0], points), jnp.float32)] * with_terms + [
        jax.ShapeDtypeStruct((1, points), jnp.float32),
        jax.ShapeDtypeStruct(own, jnp.float32),
        jax.ShapeDtypeStruct(own, jnp.bfloat16),
    ]
    kernel = functools.partial(last_kernel, len(normals))
    return local_call(kernel, "last", outs, [*rows, unit, live, *normals], 4)


def blend_kernel(blocks, *refs):
    terms, tables, factor, out = refs[:blocks], refs[blocks:-2], refs[-2], refs[-1]
    total = jnp.zeros(out.shape, jnp.float32)
    for block, table in zip(terms, tables):
        weights = (block[...] * factor[...]).astype(jnp.bfloat16)
        total = total + lax.dot_general(
            weights, table[...], (((0,), (0,)), ((), ())), preferred_element_type=jnp.float32
        )
    out[...] = total.astype(jnp.bfloat16)


def blend(terms, tables, factor, tile):
    blocks, points = len(terms), factor.shape[1]
    tables = [jnp.concatenate(t) for t in tables]
    width = tables[0].shape[1]
    return pl.pallas_call(
        functools.partial(blend_kernel, blocks),
        grid=(points // tile,),
        out_shape=jax.ShapeDtypeStruct((points, width), jnp.bfloat16),
        in_specs=[pl.BlockSpec((t.shape[0], tile), lambda i: (0, i)) for t in terms]
        + [pl.BlockSpec(t.shape, lambda i: (0, 0)) for t in tables]
        + [pl.BlockSpec((1, tile), lambda i: (0, i))],
        out_specs=pl.BlockSpec((tile, width), lambda i: (i, 0)),
        name="blend",
        compiler_params=VMEM_ROOM,
        cost_estimate=cost(16),
    )(*terms, *tables, factor)


def low_bit(number):
    return number & -number


def offset(j):
    return j ^ (j >> 1) ^ (j >> 2) ^ (j >> 3) ^ (j >> 4)


def step(values, j):
    return swap(values, 2 * offset(j))


def bits_of(chips):
    return [1 << b for b in range(chips.bit_length() - 1)]


def gather_terms(own, unit, chips):
    rows = {0: own}
    for bit in reversed(bits_of(chips)):
        for j in sorted(rows):
            rows[j ^ bit] = step(rows[j], bit)
    tables, terms = {}, {}
    for j in range(chips):
        held = after(rows[j], *terms.values()) if j == chips - 1 else rows[j]
        tables[j] = [rows[j], swap(held, 1)]
        if j < chips - 1:
            terms[j] = scores_of(tables[j], unit)
    return tables, terms


def scatter_sums(terms, factor, first, unit, chips, beside):
    order = sorted(range(chips), key=lambda j: (low_bit(j) or chips, -j))
    kept, given, totals, gate = {}, {}, {}, ()
    for place, j in enumerate(order):
        if place:
            kept[j], given[j] = sums_of(after(terms[j], *gate), factor, unit)
        else:
            kept[j], given[j] = first
        if j:
            totals[j] = kept[j] + swap(given[j], 1).astype(jnp.float32)
        gate = (totals[order[0]],) if place else (given[j],)
    got = {}
    for j in order:
        if j > 1:
            bit, gate = low_bit(j), totals[j]
            got[j] = step(totals[j].astype(jnp.bfloat16), bit).astype(jnp.float32)
            if j ^ bit:
                totals[j ^ bit] = totals[j ^ bit] + got.pop(j)
    near = step(after(totals[1].astype(jnp.bfloat16), given[0]), 1).astype(jnp.float32)
    done = beside(gate)
    mine = kept[0] + swap(after(given[0], *done), 1).astype(jnp.float32) + near
    return mine + sum(got.values()), done


def body(points, centroids, tile_counts):
    slot_count = points.shape[1] // TILE
    shard_count = lax.axis_size("shard")
    shard_place = lax.axis_index("shard")
    group_index = lax.axis_index("grp")
    chips = shard_count // 2
    own_held = held_tiles(
        pick_entry(tile_counts, group_index), shard_place, shard_count, slot_count
    )
    live = live_row(own_held, slot_count * TILE)
    unit = rms_unit(after(points[0], live).astype(jnp.float32)).astype(jnp.bfloat16)
    current = centroids[0]
    for iteration in range(ITERS):
        tables, scored = gather_terms(current, unit, chips)
        terms = {j: scored[j][0] for j in scored}
        normals = [scored[j][1] for j in sorted(scored)]
        is_last = iteration == ITERS - 1
        *kept_terms, factor, kept, given = last_block(tables[chips - 1], unit, live, normals, is_last)
        if is_last:
            terms[chips - 1] = kept_terms[0]

        def posterior(gate):
            if not is_last:
                return ()
            blocks = sorted(tables)
            return (
                blend([after(terms[j], gate) for j in blocks], [tables[j] for j in blocks], factor, 2 * TILE),
            )

        reduced, out_rows = scatter_sums(terms, factor, (kept, given), unit, chips, posterior)
        updated = rms_unit(reduced)
        current = updated.astype(jnp.bfloat16)
    return (updated[None], out_rows[0][None])


def solution(mesh):
    return jax.shard_map(
        body,
        mesh=mesh,
        in_specs=(P("grp", "shard", None), P("grp", "shard", None), P()),
        out_specs=(P("grp", "shard", None), P("grp", "shard", None)),
        check_vma=False,
    )
```
